256 devices in a mesh: ctx: 32 (over z, y_hi, core), head: 8 (over y_lo, x).
Axes of the slice: x: 4, y: 4 (y_hi: 2, y_lo: 2; y = y_hi * 2 + y_lo), z: 8, core: 2. Of those that a mesh axis runs over, the one named last changes fastest.
Arguments:
- queries: bfloat16 [16384, 3072], P(('ctx', 'head')), may hold values from -6 to 6
- keys: bfloat16 [16384, 3072], P(('ctx', 'head')), may hold values from -6 to 6
- values: bfloat16 [16384, 3072], P(('ctx', 'head')), may hold values from -6 to 6
- span_tiles: int32 [4], replicated, may hold values from 1 to 48, 128 in all
Outputs:
- attended: bfloat16 [16384, 3072], P(('ctx', 'head'))
The draws below stay inside these ranges and needn't reach their ends.
Inputs may be any that keep to these rules, and one draw needn't show every extreme that they name: `span_tiles`: the entries sum to 128; the longest span has exactly 48 tiles.
All inputs are finite; a program needn't handle non-finite values.
Results may differ from the reference program's by a relative error of at most 0.0075.
Values may be sent and summed in bfloat16 or wider, within the bound.
No kernel may reach another device: no remote copies, remote signals or barrier semaphores. Data moves between devices by JAX's collectives and lax.ppermute only.
A program may use at most 128 MiB of HBM per device.

```python
import math
import jax
import jax.numpy as jnp
import numpy as np
from jax import lax

HEADS = 24
HD = 128
TILE = 128
SPANS = 4
TOKENS = 16384
NTILES = 128
MOST = 48


def draw_queries(key, part):
    key = jax.random.fold_in(key, 7)
    return jax.random.truncated_normal(key, -4.0, 4.0, (TOKENS, HEADS * HD), jnp.float32).astype(jnp.bfloat16)


def draw_keys(key, part):
    key = jax.random.fold_in(key, 13)
    return jax.random.truncated_normal(key, -4.0, 4.0, (TOKENS, HEADS * HD), jnp.float32).astype(jnp.bfloat16)


def shard_levels(own_key, dims, shards, low, largest):
    gain, own = 1.0, jax.random.fold_in(own_key, 6)
    for dim, shards_of in shards:
        draws = jnp.exp(jax.random.uniform(jax.random.fold_in(own, dim), (shards_of,), jnp.float32, low / len(shards), largest / len(shards)))
        gain = gain * jnp.repeat(draws, dims[dim] // shards_of).reshape([-1 if axis == dim else 1 for axis in range(len(dims))])
    return gain


def length_profile(number_of, total, bound, slope):
    portions = [(1 << 20) // math.isqrt(grade ** slope) + 1 for grade in range(2, number_of + 1)]
    surplus, counts = total - bound - (number_of - 1), [1] * (number_of - 1)
    while surplus > 0:
        candidates = [i for i in range(number_of - 1) if counts[i] < bound]
        mass, remaining = sum([portions[i] for i in candidates]), surplus
        for i in candidates:
            addition = min(bound - counts[i], max(1, remaining * portions[i] // mass), surplus)
            counts[i] = counts[i] + addition
            surplus = surplus - addition
    return np.array([bound] + counts)


def uneven_parts(rng, amount, total, most, skew):
    if amount == 2:
        one = jax.random.randint(rng, (), max(1, total - most), min(most, total - 1) + 1)
        return jnp.stack([one, total - one])
    sizes = jnp.asarray(length_profile(amount, total, most, skew), jnp.int32)
    pairs = (amount - 1) // 2
    donor, sink = sizes[1:1 + 2 * pairs:2], sizes[2:2 + 2 * pairs:2]
    room = jnp.minimum(donor - 1, most - sink)
    shifted = jax.random.randint(jax.random.fold_in(rng, 1), (pairs,), 0, 1 << 20) % (room + 1)
    sizes = sizes.at[1:1 + 2 * pairs:2].set(donor - shifted).at[2:2 + 2 * pairs:2].set(sink + shifted)
    return sizes[jax.random.permutation(jax.random.fold_in(rng, 2), amount)]


def scatter_about(own_key, dims, width, reach, cuts=(), kind=jnp.bfloat16):
    values = width * jax.random.normal(own_key, dims, jnp.float32)
    if cuts:
        values = values * shard_levels(own_key, dims, cuts, -0.22, 0.18)
    return jnp.clip(values, -reach, reach).astype(kind)


def setup_inputs(seed: int = 0) -> dict:
    key_of = jax.random.split(jax.random.key(seed), 5)
    return {
        "queries": draw_queries(jax.random.fold_in(key_of[4], 71), 0),
        "keys": draw_keys(jax.random.fold_in(key_of[4], 71), 0),
        "values": scatter_about(key_of[2], (TOKENS, HEADS * HD), 1.0, 6.0, ((0, 256),)),
        "span_tiles": uneven_parts(key_of[3], SPANS, NTILES, MOST, 1).astype(jnp.int32),
    }


neg_large = -1.0e30


def reference(queries, keys, values, span_tiles):
    ends = jnp.cumsum(span_tiles.astype(jnp.int32)) * TILE
    bounds = ends[:SPANS - 1].astype(jnp.int32)
    positions = jnp.arange(TOKENS, dtype=jnp.int32)
    token_span = jnp.sum((positions[:, None] >= bounds[None, :]).astype(jnp.int32), axis=1)
    qblock = math.gcd(TOKENS, 512)
    nblocks = TOKENS // qblock
    scale = HD ** -0.5
    q_heads = queries.reshape(TOKENS, HEADS, HD).transpose(1, 0, 2)
    k_heads = keys.reshape(TOKENS, HEADS, HD).transpose(1, 0, 2)
    v_heads = values.reshape(TOKENS, HEADS, HD).transpose(1, 0, 2)

    def one_head(operands):
        q_head, k_head, v_head = operands

        def one_block(index):
            start = (index * qblock).astype(jnp.int32)
            q_rows = lax.dynamic_slice_in_dim(q_head, start, qblock, 0)
            q_span = lax.dynamic_slice_in_dim(token_span, start, qblock, 0)
            scores = jnp.dot(q_rows, k_head.T, preferred_element_type=jnp.float32) * scale
            allowed = token_span[None, :] <= q_span[:, None]
            scores = jnp.where(allowed, scores, neg_large)
            top = jnp.max(scores, axis=1, keepdims=True)
            weights = jnp.where(allowed, jnp.exp(scores - top), 0.0)
            total = jnp.sum(weights, axis=1, keepdims=True)
            mixed = jnp.dot(weights.astype(jnp.bfloat16), v_head, preferred_element_type=jnp.float32)
            return (mixed / total).astype(jnp.bfloat16)

        blocks = lax.map(one_block, jnp.arange(nblocks, dtype=jnp.int32))
        return blocks.reshape(TOKENS, HD)

    result = lax.map(one_head, (q_heads, k_heads, v_heads))
    return result.transpose(1, 0, 2).reshape(TOKENS, HEADS * HD)
```

```python
import jax
import jax.numpy as jnp
from jax import lax
from jax.experimental import pallas as pl
from jax.experimental.pallas import tpu as pltpu
from jax.sharding import Mesh, PartitionSpec as P

HD = 128
TILE = 128
SPANS = 4
Z, YH, CORES, YL, X = 8, 2, 2, 2, 4
Y = YH * YL
TOK = 64
HEADS_HERE = 3
QT = Y * TOK
KT = X * TOK
CHUNKS = Z * CORES
GROUP = 4
VROWS = HD + 16
LOW = -1e30
FLOOR = -1e20
FACTOR = HD ** (-0.5) * 1.4426950408889634
ALL = ("z", "yh", "c", "yl", "x")


def pack_kernel(q_ref, k_ref, v_ref, *outs):
    for head in range(HEADS_HERE):
        for plane in range(Z):
            lo = (plane * HEADS_HERE + head) * HD
            for which, ref in enumerate((q_ref, k_ref, v_ref)):
                outs[head][plane, which * TOK:(which + 1) * TOK, :] = ref[:, lo:lo + HD]


def pack(queries, keys, values):
    return pl.pallas_call(
        pack_kernel,
        out_shape=[jax.ShapeDtypeStruct((Z, 3 * TOK, HD), jnp.bfloat16)] * HEADS_HERE,
        name="pack",
    )(queries, keys, values)


def unpack_kernel(*refs):
    out = refs[-1]
    for head in range(HEADS_HERE):
        for plane in range(Z):
            lo = (plane * HEADS_HERE + head) * HD
            out[:, lo:lo + HD] = refs[head][plane]


def unpack(parts):
    return pl.pallas_call(
        unpack_kernel,
        out_shape=jax.ShapeDtypeStruct((TOK, Z * HEADS_HERE * HD), jnp.bfloat16),
        name="unpack",
    )(*parts)


def attend_kernel(info, own, q1, q2, q3, a1, a2, a3, b0, b1, b2, b3, o_ref, lse_ref,
                  k_scr, v_scr, s_scr, q_scr, limit_scr, acc_scr, top_scr, steps):
    x, y, c = info[4], info[5], info[6]
    ones = jnp.ones((VROWS - HD, KT), jnp.bfloat16)
    y_off = (y // YL) * (TOK * CORES * YL * X) + (y % YL) * KT
    lane_block = lax.broadcasted_iota(jnp.int32, (1, QT), 1) // TOK

    def chunk_start(j):
        return (j // CORES) * (TOK * 32) + (j % CORES) * (TOK * 8) + y_off

    def arrange(plane, whole):
        for e, refs in ((0, (own, a1, a2, a3)), (1, (b0, b1, b2, b3))):
            j = plane * CORES + jnp.where(e == 0, c, 1 - c)
            vs = []
            for d, ref in enumerate(refs):
                at = TOK if ref is own else 0
                k = ref[plane, at:at + TOK, :]
                k_scr[j, d * TOK:(d + 1) * TOK, 0:HD] = k
                k_scr[j, d * TOK:(d + 1) * TOK, HD:2 * HD] = k
                vs.append(ref[plane, at + TOK:at + 2 * TOK, :])
            v = jnp.concatenate(vs, axis=0)
            v_scr[j, 0:HD, :] = v.T
            v_scr[j, HD:VROWS, :] = ones
        q = jnp.concatenate([own[plane, 0:TOK, :], q1[plane], q2[plane], q3[plane]], axis=0).astype(jnp.float32) * FACTOR
        high = q.astype(jnp.bfloat16)
        low = (q - high.astype(jnp.float32)).astype(jnp.bfloat16)
        q_scr[plane, :, 0:HD] = high
        q_scr[plane, :, HD:2 * HD] = low
        limits = []
        for d in range(Y):
            yq = (y + Y - d) % Y
            tok = plane * (TOK * 32) + (yq // YL) * (TOK * 16) + c * (TOK * 8) + (yq % YL) * (TOK * 4) + x * TOK
            end = info[SPANS - 1]
            for s in range(SPANS - 2, -1, -1):
                end = jnp.where(tok < info[s], info[s], end)
            limits.append(end)
        most = jnp.maximum(jnp.maximum(limits[0], limits[1]), jnp.maximum(limits[2], limits[3]))
        far = jnp.maximum(most - y_off, 0)
        rest = far % (TOK * 32)
        seen = (far // (TOK * 32)) * CORES + (rest > 0).astype(jnp.int32) + (rest > TOK * 8).astype(jnp.int32)
        count = jnp.maximum((seen + GROUP - 1) // GROUP, 1)
        steps[plane] = count
        limit_scr[plane, 0:1, :] = jnp.where(
            lane_block == 0, limits[0],
            jnp.where(lane_block == 1, limits[1], jnp.where(lane_block == 2, limits[2], limits[3])),
        )
        acc_scr[plane] = jnp.zeros((VROWS, QT), jnp.float32)
        return whole + count

    rounds = lax.fori_loop(0, Z, arrange, jnp.int32(0))

    def bias_rows(i, j):
        start = chunk_start(j)
        limit_row = limit_scr[i, 0:1, :]
        return [jnp.where(start + ((x + X - d) % X) * TOK < limit_row, 0.0, LOW) for d in range(X)]

    def produce(i, j, slot, best):
        s = lax.dot_general(k_scr[j], q_scr[i], (((1,), (1,)), ((), ())), preferred_element_type=jnp.float32)
        s_scr[slot] = s
        for d, bias in enumerate(bias_rows(i, j)):
            part = jnp.max(s[d * TOK:(d + 1) * TOK].reshape(TOK // 8, 8, QT), axis=0) + bias
            best = jnp.maximum(best, part)
        return best

    def consume(i, j, slot, top):
        s = s_scr[slot]
        ps = []
        for d, bias in enumerate(bias_rows(i, j)):
            ps.append(jnp.exp2(s[d * TOK:(d + 1) * TOK] - (top - bias)).astype(jnp.bfloat16))
        return jnp.concatenate(ps, axis=0)

    def step(_, state):
        i, n, best, old = state
        top = jnp.max(best, axis=0, keepdims=True)
        last = n + 1 >= steps[i]
        i2 = jnp.where(last, jnp.minimum(i + 1, Z - 1), i)
        n2 = jnp.where(last, 0, n + 1)
        best = jnp.where(last, FLOOR, best)
        accum = acc_scr[i] * jnp.exp2(old - top)
        for g in range(GROUP):
            j = n * GROUP + g
            p = consume(i, j, g, top)
            best = produce(i2, n2 * GROUP + g, g, best)
            accum = accum + jnp.dot(v_scr[j], p, preferred_element_type=jnp.float32)
        acc_scr[i] = accum
        top_scr[i, 0:1, :] = top
        return i2, n2, best, jnp.where(last, FLOOR, top)

    best = jnp.full((8, QT), FLOOR, jnp.float32)
    for g in range(GROUP):
        best = produce(0, g, g, best)
    lax.fori_loop(0, rounds, step, (jnp.int32(0), jnp.int32(0), best, jnp.full((1, QT), FLOOR, jnp.float32)))
    for i in range(Z):
        total = acc_scr[i, HD:HD + 1, :]
        some = total > 0.0
        safe = jnp.where(some, total, 1.0)
        lse_ref[i:i + 1, :] = jnp.where(some, top_scr[i, 0:1, :] + jnp.log2(safe), LOW)
        out = (acc_scr[i, 0:HD, :] * (1.0 / safe)).T.astype(jnp.bfloat16)
        for d in range(Y):
            o_ref[d, i] = out[d * TOK:(d + 1) * TOK]


def attend(info, own, qs, firsts, others):
    pairs = Z * QT * CHUNKS * KT
    return pl.pallas_call(
        attend_kernel,
        in_specs=[pl.BlockSpec(memory_space=pltpu.SMEM)] + [pl.BlockSpec(memory_space=pltpu.VMEM)] * 11,
        out_specs=[pl.BlockSpec(memory_space=pltpu.VMEM)] * 2,
        out_shape=[
            jax.ShapeDtypeStruct((Y, Z, TOK, HD), jnp.bfloat16),
            jax.ShapeDtypeStruct((Z, QT), jnp.float32),
        ],
        scratch_shapes=[
            pltpu.VMEM((CHUNKS, KT, 2 * HD), jnp.bfloat16),
            pltpu.VMEM((CHUNKS, VROWS, KT), jnp.bfloat16),
            pltpu.VMEM((GROUP, KT, QT), jnp.float32),
            pltpu.VMEM((Z, QT, 2 * HD), jnp.bfloat16),
            pltpu.VMEM((Z, 8, QT), jnp.int32),
            pltpu.VMEM((Z, VROWS, QT), jnp.float32),
            pltpu.VMEM((Z, 8, QT), jnp.float32),
            pltpu.SMEM((Z,), jnp.int32),
        ],
        compiler_params=pltpu.CompilerParams(vmem_limit_bytes=32 * 1024 * 1024),
        cost_estimate=pl.CostEstimate(flops=4 * pairs * HD, bytes_accessed=4 << 20, transcendentals=pairs),
        name="attend",
    )(info, own, *qs, *firsts, *others)


def turn(array, axis, size, by):
    return lax.ppermute(array, axis, [(i, (i + by) % size) for i in range(size)])


def body(queries, keys, values, span_tiles):
    x, c = lax.axis_index("x"), lax.axis_index("c")
    y = lax.axis_index("yh") * YL + lax.axis_index("yl")
    ends = jnp.cumsum(span_tiles).astype(jnp.int32) * TILE
    info = jnp.concatenate([ends, jnp.stack([x, y, c, c]).astype(jnp.int32)])
    packed = pack(queries, keys, values)
    parts = []
    for head in range(HEADS_HERE):
        own = lax.all_to_all(packed[head], "z", split_axis=0, concat_axis=0, tiled=True)
        kv, q = own[:, TOK:, :], own[:, :TOK, :]
        firsts = [turn(kv, "x", X, d) for d in range(1, X)]
        others = [lax.ppermute(item, "c", [(0, 1), (1, 0)]) for item in [kv] + firsts]
        qs = [turn(q, ("yh", "yl"), Y, d) for d in range(1, Y)]
        out, lse = attend(info, own, qs, firsts, others)
        outs = [out[0]] + [turn(out[d], ("yh", "yl"), Y, -d) for d in range(1, Y)]
        stats = [lse] + [turn(lse, ("yh", "yl"), Y, -d) for d in range(1, Y)]
        stats = [item[:, d * TOK:(d + 1) * TOK] for d, item in enumerate(stats)]
        top = jnp.maximum(jnp.maximum(stats[0], stats[1]), jnp.maximum(stats[2], stats[3]))
        weights = [jnp.exp2(item - top) for item in stats]
        total = weights[0] + weights[1] + weights[2] + weights[3]
        mixed = sum((w / total)[:, :, None] * o.astype(jnp.float32) for w, o in zip(weights, outs))
        parts.append(lax.all_to_all(mixed.astype(jnp.bfloat16), "z", split_axis=0, concat_axis=0, tiled=True))
    return unpack(parts)


def solution(mesh):
    fine = Mesh(mesh.devices.reshape(Z, YH, CORES, YL, X), ALL)
    return jax.shard_map(
        body,
        mesh=fine,
        in_specs=(P(ALL, None), P(ALL, None), P(ALL, None), P()),
        out_specs=P(ALL, None),
        check_vma=False,
    )
```

```python
import functools

import jax
import jax.numpy as jnp
from jax import lax
from jax.experimental import pallas as pl
from jax.experimental.pallas import tpu as pltpu
from jax.sharding import Mesh, PartitionSpec as P

HD = 128
TILE = 128
SPANS = 4
Z, YH, CORES, YL, X = 8, 2, 2, 2, 4
Y = YH * YL
TOK = 64
HALF = TOK // 2
HEADS_HERE = 3
QT = Y * TOK
KT = X * TOK
CHUNKS = Z * CORES
GROUP = 4
VROWS = HD + 16
LOW = -1e30
FLOOR = -1e20
FACTOR = HD ** (-0.5) * 1.4426950408889634
ALL = ("z", "yh", "c", "yl", "x")


def pack_kernel(q_ref, k_ref, v_ref, most, rest):
    for plane in range(Z):
        for core in range(CORES):
            to = plane * CORES + core
            half = slice(core * HALF, (core + 1) * HALF)
            shared = slice(plane * HEADS_HERE * HD, (plane * HEADS_HERE + 1) * HD)
            lo = (plane * HEADS_HERE + 1 + core) * HD
            own = slice(lo, lo + HD)
            most[to, 0:TOK, :] = k_ref[:, own]
            most[to, TOK:2 * TOK, :] = v_ref[:, own]
            most[to, 2 * TOK:3 * TOK, :] = q_ref[:, own]
            most[to, 3 * TOK:3 * TOK + HALF, :] = q_ref[half, shared]
            rest[to, 0:HALF, :] = k_ref[half, shared]
            rest[to, HALF:TOK, :] = v_ref[half, shared]


def pack(queries, keys, values):
    return pl.pallas_call(
        pack_kernel,
        out_shape=[
            jax.ShapeDtypeStruct((CHUNKS, 3 * TOK + HALF, HD), jnp.bfloat16),
            jax.ShapeDtypeStruct((CHUNKS, TOK, HD), jnp.bfloat16),
        ],
        name="pack",
    )(queries, keys, values)


def unpack_kernel(ref, out):
    for plane in range(Z):
        for core in range(CORES):
            at = plane * CORES + core
            lo = (plane * HEADS_HERE + 1 + core) * HD
            out[:, lo:lo + HD] = ref[at, 0:TOK, :]
            lo = plane * HEADS_HERE * HD
            out[core * HALF:(core + 1) * HALF, lo:lo + HD] = ref[at, TOK:TOK + HALF, :]


def unpack(parts):
    return pl.pallas_call(
        unpack_kernel,
        out_shape=jax.ShapeDtypeStruct((TOK, Z * HEADS_HERE * HD), jnp.bfloat16),
        name="unpack",
    )(parts)


def attend_kernel(shared, planes, join, span_tiles, *refs):
    qs, refs = refs[:Y], refs[Y:]
    mine, refs = (refs[:CORES], refs[CORES:]) if shared else (refs[:X], refs[X:])
    o_refs, refs = refs[:Y], refs[Y:]
    k_scr, v_scr, s_scr, q_scr, limit_scr, acc_scr, top_scr, steps, q_in, v_in, o_scr, sems = refs
    x = lax.axis_index("x")
    y = lax.axis_index("yh") * YL + lax.axis_index("yl")
    bounds = [span_tiles[0] * TILE]
    for s in range(1, SPANS):
        bounds.append(bounds[-1] + span_tiles[s] * TILE)

    copies = [[], [], []]

    def fetch(kind, source, target):
        copy = pltpu.make_async_copy(source, target, sems.at[sum(map(len, copies))])
        copy.start()
        copies[kind].append(copy)

    for d in range(Y):
        at = pl.ds(TOK, HALF) if shared else pl.ds(0, TOK)
        fetch(0, qs[d].at[:, at, :], q_in.at[d])
    size = HALF if shared else TOK
    for d in range(X):
        sources = [ref.at[(x + X - d) % X] for ref in mine] if shared else [mine[d]]
        for e, source in enumerate(sources):
            at = pl.ds(d * TOK + e * HALF, size)
            fetch(1, source.at[:, pl.ds(size, size), :], v_in.at[:, at, :])
            for twice in range(2):
                fetch(2, source.at[:, pl.ds(0, size), :], k_scr.at[:, at, pl.ds(twice * HD, HD)])

    tiles = planes // join
    wide = join * QT
    ones = jnp.ones((VROWS - HD, KT), jnp.bfloat16)
    y_off = (y // YL) * (TOK * CORES * YL * X) + (y % YL) * KT
    lane = lax.broadcasted_iota(jnp.int32, (1, QT), 1)
    rows = planes * TOK

    def chunk_start(j):
        return (j // CORES) * (TOK * 32) + (j % CORES) * (TOK * 8) + y_off

    def arrange_values(j, carry):
        v_scr[j, 0:HD, :] = v_in[j].T
        v_scr[j, HD:VROWS, :] = ones
        return carry

    def arrange_queries(t, whole):
        most = jnp.int32(0)
        for part in range(join):
            i = t * join + part
            parts = []
            for d in range(Y):
                if shared:
                    parts += [q_in[d, i * CORES + e] for e in range(CORES)]
                else:
                    parts.append(q_in[d, i])
            q = jnp.concatenate(parts, axis=0).astype(jnp.float32) * FACTOR
            high = q.astype(jnp.bfloat16)
            low = (q - high.astype(jnp.float32)).astype(jnp.bfloat16)
            at = slice(part * QT, (part + 1) * QT)
            q_scr[t, at, 0:HD] = high
            q_scr[t, at, HD:2 * HD] = low
            row = jnp.zeros((1, QT), jnp.int32)
            for block in range(QT // size):
                yq = (y + Y - (block * size) // TOK) % Y
                j = i * CORES + block % CORES if shared else i
                tok = (j // CORES) * (TOK * 32) + (yq // YL) * (TOK * 16) + (j % CORES) * (TOK * 8) + (yq % YL) * (TOK * 4) + x * TOK
                end = bounds[SPANS - 1]
                for s in range(SPANS - 2, -1, -1):
                    end = jnp.where(tok < bounds[s], bounds[s], end)
                most = jnp.maximum(most, end)
                row = jnp.where(lane >= block * size, end, row)
            limit_scr[t, 0:1, at] = row
        far = jnp.maximum(most - y_off, 0)
        rest = far % (TOK * 32)
        seen = (far // (TOK * 32)) * CORES + (rest > 0).astype(jnp.int32) + (rest > TOK * 8).astype(jnp.int32)
        count = jnp.maximum((seen + GROUP - 1) // GROUP, 1)
        steps[t] = count
        acc_scr[t] = jnp.zeros((VROWS, wide), jnp.float32)
        return whole + count

    for copy in copies[0]:
        copy.wait()
    rounds = lax.fori_loop(0, tiles, arrange_queries, jnp.int32(0))
    for copy in copies[1]:
        copy.wait()
    lax.fori_loop(0, CHUNKS, arrange_values, 0)
    for copy in copies[2]:
        copy.wait()

    def bias_rows(t, j):
        start = chunk_start(j)
        limit_row = limit_scr[t, 0:1, :]
        return [jnp.where(start + ((x + X - d) % X) * TOK < limit_row, 0.0, LOW) for d in range(X)]

    def produce(t, j, slot, best):
        s = lax.dot_general(k_scr[j], q_scr[t], (((1,), (1,)), ((), ())), preferred_element_type=jnp.float32)
        s_scr[slot] = s
        for d, bias in enumerate(bias_rows(t, j)):
            part = jnp.max(s[d * TOK:(d + 1) * TOK].reshape(TOK // 8, 8, wide), axis=0) + bias
            best = jnp.maximum(best, part)
        return best

    def consume(t, j, slot, top):
        s = s_scr[slot]
        ps = []
        for d, bias in enumerate(bias_rows(t, j)):
            ps.append(jnp.exp2(s[d * TOK:(d + 1) * TOK] - (top - bias)).astype(jnp.bfloat16))
        return jnp.concatenate(ps, axis=0)

    def step(_, state):
        t, n, best, old = state
        top = jnp.max(best, axis=0, keepdims=True)
        last = n + 1 >= steps[t]
        t2 = jnp.where(last, jnp.minimum(t + 1, tiles - 1), t)
        n2 = jnp.where(last, 0, n + 1)
        best = jnp.where(last, FLOOR, best)
        accum = acc_scr[t] * jnp.exp2(old - top)
        for g in range(GROUP):
            j = n * GROUP + g
            p = consume(t, j, g, top)
            best = produce(t2, n2 * GROUP + g, g, best)
            accum = accum + jnp.dot(v_scr[j], p, preferred_element_type=jnp.float32)
        acc_scr[t] = accum
        top_scr[t, 0:1, :] = top
        return t2, n2, best, jnp.where(last, FLOOR, top)

    best = jnp.full((8, wide), FLOOR, jnp.float32)
    for g in range(GROUP):
        best = produce(0, g, g, best)
    lax.fori_loop(0, rounds, step, (jnp.int32(0), jnp.int32(0), best, jnp.full((1, wide), FLOOR, jnp.float32)))
    stats = []
    for i in range(planes):
        t, at = i // join, slice(i % join * QT, (i % join + 1) * QT)
        total = acc_scr[t, HD:HD + 1, at]
        some = total > 0.0
        safe = jnp.where(some, total, 1.0)
        stats.append(jnp.where(some, top_scr[t, 0:1, at] + jnp.log2(safe), LOW))
        out = (acc_scr[t, 0:HD, at] * (1.0 / safe)).T.astype(jnp.bfloat16)
        for d in range(Y):
            o_scr[d, i * TOK:(i + 1) * TOK, :] = out[d * TOK:(d + 1) * TOK]
    lse = jnp.concatenate(stats, axis=0)
    high = lse.astype(jnp.bfloat16)
    lse = lse - high.astype(jnp.float32)
    middle = lse.astype(jnp.bfloat16)
    low = (lse - middle.astype(jnp.float32)).astype(jnp.bfloat16)
    for d in range(Y):
        at = slice(d * TOK, (d + 1) * TOK)
        first = jnp.concatenate([high[:, at], middle[:, at]], axis=1)
        second = jnp.concatenate([low[:, at], jnp.zeros((planes, HD - TOK), jnp.bfloat16)], axis=1)
        o_scr[d, rows:rows + 2 * planes, :] = jnp.concatenate([first, second], axis=0)
    out_copies = [pltpu.make_async_copy(o_scr.at[d], o_refs[d], sems.at[d]) for d in range(Y)]
    for copy in out_copies:
        copy.start()
    for copy in out_copies:
        copy.wait()


def attend(span_tiles, shared, qs, mine):
    planes = Z if shared else CHUNKS
    join = 2 if shared else 4
    tiles, wide = planes // join, join * QT
    pairs = planes * QT * CHUNKS * KT
    arrays = [*qs, *mine]
    return pl.pallas_call(
        functools.partial(attend_kernel, shared, planes, join),
        in_specs=[pl.BlockSpec(memory_space=pltpu.SMEM)] + [pl.BlockSpec(memory_space=pl.ANY)] * len(arrays),
        out_specs=[pl.BlockSpec(memory_space=pl.ANY)] * Y,
        out_shape=[jax.ShapeDtypeStruct((planes * (TOK + 2), HD), jnp.bfloat16)] * Y,
        scratch_shapes=[
            pltpu.VMEM((CHUNKS, KT, 2 * HD), jnp.bfloat16),
            pltpu.VMEM((CHUNKS, VROWS, KT), jnp.bfloat16),
            pltpu.VMEM((GROUP, KT, wide), jnp.float32),
            pltpu.VMEM((tiles, wide, 2 * HD), jnp.bfloat16),
            pltpu.VMEM((tiles, 8, wide), jnp.int32),
            pltpu.VMEM((tiles, VROWS, wide), jnp.float32),
            pltpu.VMEM((tiles, 8, wide), jnp.float32),
            pltpu.SMEM((tiles,), jnp.int32),
            pltpu.VMEM((Y, CHUNKS, HALF if shared else TOK, HD), jnp.bfloat16),
            pltpu.VMEM((CHUNKS, KT, HD), jnp.bfloat16),
            pltpu.VMEM((Y, planes * (TOK + 2), HD), jnp.bfloat16),
            pltpu.SemaphoreType.DMA((Y + 3 * X * (2 if shared else 1),)),
        ],
        compiler_params=pltpu.CompilerParams(vmem_limit_bytes=30 * 1024 * 1024),
        cost_estimate=pl.CostEstimate(flops=8 * pairs * HD, bytes_accessed=4 << 20, transcendentals=pairs),
        name="attend_shared" if shared else "attend_own",
    )(span_tiles, *arrays)


def turn(array, axis, size, by):
    return lax.ppermute(array, axis, [(i, (i + by) % size) for i in range(size)])


def after(array, *earlier):
    return lax.optimization_barrier((array, *earlier))[0]


def along_z(array):
    return lax.all_to_all(array, ("z", "c"), split_axis=0, concat_axis=0, tiled=True)


def combine(outs):
    tiles = outs[0].shape[0] // (TOK + 2)
    rows = tiles * TOK
    stats = []
    for item in outs:
        three = item[rows:].astype(jnp.float32)
        stats.append(three[:tiles, :TOK] + three[:tiles, TOK:] + three[tiles:, :TOK])
    top = jnp.maximum(jnp.maximum(stats[0], stats[1]), jnp.maximum(stats[2], stats[3]))
    weights = [jnp.exp2(item - top) for item in stats]
    total = weights[0] + weights[1] + weights[2] + weights[3]
    mixed = sum(
        (w / total)[:, :, None] * item[:rows].reshape(tiles, TOK, HD).astype(jnp.float32)
        for w, item in zip(weights, outs)
    )
    return mixed.astype(jnp.bfloat16).reshape(CHUNKS, -1, HD)


def body(queries, keys, values, span_tiles):
    def spread(array):
        return [turn(array, "x", X, d) for d in range(1, X)]

    def exchange(out):
        return [out[0]] + [turn(out[d], ("yh", "yl"), Y, -d) for d in range(1, Y)]

    most, rest = pack(queries, keys, values)
    most = along_z(most)
    rest = along_z(after(rest, most))
    mine = [most] + spread(most[:, :2 * TOK])
    q = most[:, 2 * TOK:]
    qs = [q] + [turn(q, ("yh", "yl"), Y, d) for d in range(1, Y - 1)]
    qs.append(turn(after(q, qs[1]), ("yh", "yl"), Y, Y - 1))
    mine2 = lax.all_to_all(
        jnp.broadcast_to(rest, (X, *rest.shape)), "x", split_axis=0, concat_axis=0, tiled=True
    )
    own_out = attend(span_tiles, False, qs, mine)
    others = lax.ppermute(after(mine2, own_out), "c", [(0, 1), (1, 0)])
    got = exchange(own_out)
    shared_out = attend(span_tiles, True, qs, [mine2, others])
    mixed = combine(after(got, shared_out))
    mixed2 = combine(exchange(shared_out))
    return unpack(along_z(jnp.concatenate([mixed, mixed2], axis=1)))


def solution(mesh):
    fine = Mesh(mesh.devices.reshape(Z, YH, CORES, YL, X), ALL)
    return jax.shard_map(
        body,
        mesh=fine,
        in_specs=(P(ALL, None), P(ALL, None), P(ALL, None), P()),
        out_specs=P(ALL, None),
        check_vma=False,
    )
```

```python
import functools

import jax
import jax.numpy as jnp
from jax import lax
from jax.experimental import pallas as pl
from jax.experimental.pallas import tpu as pltpu
from jax.sharding import Mesh, PartitionSpec as P

HD = 128
TILE = 128
SPANS = 4
Z, YH, CORES, YL, X = 8, 2, 2, 2, 4
Y = YH * YL
TOK = 64
HALF = TOK // 2
HEADS_HERE = 3
QT = Y * TOK
KT = X * TOK
PLANES = 4
CHUNKS = Z * CORES
GROUP = 4
VROWS = HD + 16
LOW = -1e30
FLOOR = -1e20
FACTOR = HD ** (-0.5) * 1.4426950408889634
ALL = ("z", "yh", "c", "yl", "x")


def pack_kernel(q_ref, k_ref, v_ref, most, rest):
    for plane in range(PLANES):
        for core in range(CORES):
            to = plane * CORES + core
            half = slice(core * HALF, (core + 1) * HALF)
            shared = slice(plane * HEADS_HERE * HD, (plane * HEADS_HERE + 1) * HD)
            lo = (plane * HEADS_HERE + 1 + core) * HD
            own = slice(lo, lo + HD)
            most[to, 0:TOK, :] = k_ref[:, own]
            most[to, TOK:2 * TOK, :] = v_ref[:, own]
            most[to, 2 * TOK:3 * TOK, :] = q_ref[:, own]
            most[to, 3 * TOK:3 * TOK + HALF, :] = q_ref[half, shared]
            rest[to, 0:HALF, :] = k_ref[half, shared]
            rest[to, HALF:TOK, :] = v_ref[half, shared]


def pack(queries, keys, values):
    blocks = [(PLANES * CORES, 3 * TOK + HALF, HD), (PLANES * CORES, TOK, HD)]
    return pl.pallas_call(
        pack_kernel,
        grid=(Z // PLANES,),
        in_specs=[pl.BlockSpec((TOK, PLANES * HEADS_HERE * HD), lambda i: (0, i))] * 3,
        out_specs=[pl.BlockSpec(block, lambda i: (i, 0, 0)) for block in blocks],
        out_shape=[
            jax.ShapeDtypeStruct((CHUNKS, 3 * TOK + HALF, HD), jnp.bfloat16),
            jax.ShapeDtypeStruct((CHUNKS, TOK, HD), jnp.bfloat16),
        ],
        name="pack",
    )(queries, keys, values)


def unpack_kernel(ref, out):
    for plane in range(PLANES):
        for core in range(CORES):
            at = plane * CORES + core
            lo = (plane * HEADS_HERE + 1 + core) * HD
            out[:, lo:lo + HD] = ref[at, 0:TOK, :]
            lo = plane * HEADS_HERE * HD
            out[core * HALF:(core + 1) * HALF, lo:lo + HD] = ref[at, TOK:TOK + HALF, :]


def unpack(parts):
    return pl.pallas_call(
        unpack_kernel,
        grid=(Z // PLANES,),
        in_specs=[pl.BlockSpec((PLANES * CORES, TOK + HALF, HD), lambda i: (i, 0, 0))],
        out_specs=pl.BlockSpec((TOK, PLANES * HEADS_HERE * HD), lambda i: (0, i)),
        out_shape=jax.ShapeDtypeStruct((TOK, Z * HEADS_HERE * HD), jnp.bfloat16),
        name="unpack",
    )(parts)


def attend_kernel(shared, planes, join, span_tiles, *refs):
    qs, refs = refs[:Y], refs[Y:]
    mine, refs = (refs[:CORES], refs[CORES:]) if shared else (refs[:X], refs[X:])
    o_refs, refs = refs[:Y], refs[Y:]
    k_scr, v_scr, s_scr, q_scr, limit_scr, acc_scr, top_scr, steps, q_in, v_in, sems = refs
    x = lax.axis_index("x")
    y = lax.axis_index("yh") * YL + lax.axis_index("yl")
    bounds = [span_tiles[0] * TILE]
    for s in range(1, SPANS):
        bounds.append(bounds[-1] + span_tiles[s] * TILE)

    copies = [[], [], []]

    def fetch(kind, source, target):
        copy = pltpu.make_async_copy(source, target, sems.at[sum(map(len, copies))])
        copy.start()
        copies[kind].append(copy)

    for d in range(Y):
        at = pl.ds(TOK, HALF) if shared else pl.ds(0, TOK)
        fetch(0, qs[d].at[:, at, :], q_in.at[d])
    size = HALF if shared else TOK
    for d in range(X):
        sources = [ref.at[(x + X - d) % X] for ref in mine] if shared else [mine[d]]
        for e, source in enumerate(sources):
            at = pl.ds(d * TOK + e * HALF, size)
            fetch(1, source.at[:, pl.ds(size, size), :], v_in.at[:, at, :])
            for twice in range(2):
                fetch(2, source.at[:, pl.ds(0, size), :], k_scr.at[:, at, pl.ds(twice * HD, HD)])

    tiles = planes // join
    wide = join * QT
    ones = jnp.ones((VROWS - HD, KT), jnp.bfloat16)
    y_off = (y // YL) * (TOK * CORES * YL * X) + (y % YL) * KT
    lane = lax.broadcasted_iota(jnp.int32, (1, QT), 1)
    rows = planes * TOK

    def chunk_start(j):
        return (j // CORES) * (TOK * 32) + (j % CORES) * (TOK * 8) + y_off

    def arrange_values(m, carry):
        for g in range(GROUP):
            v_scr[m, 0:HD, g * KT:(g + 1) * KT] = v_in[m * GROUP + g].T
            v_scr[m, HD:VROWS, g * KT:(g + 1) * KT] = ones
        return carry

    def arrange_queries(t, whole):
        most = jnp.int32(0)
        for part in range(join):
            i = t * join + part
            parts = []
            for d in range(Y):
                if shared:
                    parts += [q_in[d, i * CORES + e] for e in range(CORES)]
                else:
                    parts.append(q_in[d, i])
            q = jnp.concatenate(parts, axis=0).astype(jnp.float32) * FACTOR
            high = q.astype(jnp.bfloat16)
            low = (q - high.astype(jnp.float32)).astype(jnp.bfloat16)
            at = slice(part * QT, (part + 1) * QT)
            q_scr[t, 0:HD, at] = high.T
            q_scr[t, HD:2 * HD, at] = low.T
            row = jnp.zeros((1, QT), jnp.int32)
            for block in range(QT // size):
                yq = (y + Y - (block * size) // TOK) % Y
                j = i * CORES + block % CORES if shared else i
                tok = (j // CORES) * (TOK * 32) + (yq // YL) * (TOK * 16) + (j % CORES) * (TOK * 8) + (yq % YL) * (TOK * 4) + x * TOK
                end = bounds[SPANS - 1]
                for s in range(SPANS - 2, -1, -1):
                    end = jnp.where(tok < bounds[s], bounds[s], end)
                most = jnp.maximum(most, end)
                row = jnp.where(lane >= block * size, end, row)
            limit_scr[t, 0:1, at] = row
        far = jnp.maximum(most - y_off, 0)
        rest = far % (TOK * 32)
        seen = (far // (TOK * 32)) * CORES + (rest > 0).astype(jnp.int32) + (rest > TOK * 8).astype(jnp.int32)
        count = jnp.maximum((seen + GROUP - 1) // GROUP, 1)
        steps[t] = count
        acc_scr[t] = jnp.zeros((VROWS, wide), jnp.float32)
        return whole + count

    for copy in copies[0]:
        copy.wait()
    rounds = lax.fori_loop(0, tiles, arrange_queries, jnp.int32(0))
    for copy in copies[1]:
        copy.wait()
    lax.fori_loop(0, CHUNKS // GROUP, arrange_values, 0)
    for copy in copies[2]:
        copy.wait()

    def bias_rows(t, j):
        start = chunk_start(j)
        limit_row = limit_scr[t, 0:1, :]
        return [jnp.where(start + ((x + X - d) % X) * TOK < limit_row, 0.0, LOW) for d in range(X)]

    def produce(t, j, slot, best):
        s = jnp.dot(k_scr[j], q_scr[t], preferred_element_type=jnp.float32)
        s_scr[slot] = s
        for d, bias in enumerate(bias_rows(t, j)):
            part = jnp.max(s[d * TOK:(d + 1) * TOK].reshape(TOK // 8, 8, wide), axis=0) + bias
            best = jnp.maximum(best, part)
        return best

    def consume(t, j, slot, top):
        s = s_scr[slot]
        ps = []
        for d, bias in enumerate(bias_rows(t, j)):
            ps.append(jnp.exp2(s[d * TOK:(d + 1) * TOK] - (top - bias)).astype(jnp.bfloat16))
        return jnp.concatenate(ps, axis=0)

    def step(_, state):
        t, n, best, old = state
        top = jnp.max(best, axis=0, keepdims=True)
        last = n + 1 >= steps[t]
        t2 = jnp.where(last, jnp.minimum(t + 1, tiles - 1), t)
        n2 = jnp.where(last, 0, n + 1)
        best = jnp.where(last, FLOOR, best)
        accum = acc_scr[t] * jnp.exp2(old - top)
        ps = []
        for g in range(GROUP):
            j = n * GROUP + g
            p = consume(t, j, g, top)
            best = produce(t2, n2 * GROUP + g, g, best)
            ps.append(p)
        acc_scr[t] = accum + jnp.dot(v_scr[n], jnp.concatenate(ps, axis=0), preferred_element_type=jnp.float32)
        top_scr[t, 0:1, :] = top
        return t2, n2, best, jnp.where(last, FLOOR, top)

    best = jnp.full((8, wide), FLOOR, jnp.float32)
    for g in range(GROUP):
        best = produce(0, g, g, best)
    lax.fori_loop(0, rounds, step, (jnp.int32(0), jnp.int32(0), best, jnp.full((1, wide), FLOOR, jnp.float32)))
    stats = []
    for i in range(planes):
        t, at = i // join, slice(i % join * QT, (i % join + 1) * QT)
        total = acc_scr[t, HD:HD + 1, at]
        some = total > 0.0
        safe = jnp.where(some, total, 1.0)
        stats.append(jnp.where(some, top_scr[t, 0:1, at] + jnp.log2(safe), LOW))
        out = (acc_scr[t, 0:HD, at] * (1.0 / safe)).T.astype(jnp.bfloat16)
        for d in range(Y):
            o_refs[d][i * TOK:(i + 1) * TOK, :] = out[d * TOK:(d + 1) * TOK]
    lse = jnp.concatenate(stats, axis=0)
    high = lse.astype(jnp.bfloat16)
    lse = lse - high.astype(jnp.float32)
    middle = lse.astype(jnp.bfloat16)
    low = (lse - middle.astype(jnp.float32)).astype(jnp.bfloat16)
    for d in range(Y):
        at = slice(d * TOK, (d + 1) * TOK)
        first = jnp.concatenate([high[:, at], middle[:, at]], axis=1)
        second = jnp.concatenate([low[:, at], jnp.zeros((planes, HD - TOK), jnp.bfloat16)], axis=1)
        o_refs[d][rows:rows + 2 * planes, :] = jnp.concatenate([first, second], axis=0)


def attend(span_tiles, shared, qs, mine):
    planes = Z if shared else CHUNKS
    join = 2 if shared else 4
    tiles, wide = planes // join, join * QT
    pairs = planes * QT * CHUNKS * KT
    arrays = [*qs, *mine]
    return pl.pallas_call(
        functools.partial(attend_kernel, shared, planes, join),
        in_specs=[pl.BlockSpec(memory_space=pltpu.SMEM)] + [pl.BlockSpec(memory_space=pl.ANY)] * len(arrays),
        out_specs=[pl.BlockSpec(memory_space=pltpu.VMEM)] * Y,
        out_shape=[pltpu.VMEM((planes * (TOK + 2), HD), jnp.bfloat16)] * Y,
        scratch_shapes=[
            pltpu.VMEM((CHUNKS, KT, 2 * HD), jnp.bfloat16),
            pltpu.VMEM((CHUNKS // GROUP, VROWS, GROUP * KT), jnp.bfloat16),
            pltpu.VMEM((GROUP, KT, wide), jnp.float32),
            pltpu.VMEM((tiles, 2 * HD, wide), jnp.bfloat16),
            pltpu.VMEM((tiles, 8, wide), jnp.int32),
            pltpu.VMEM((tiles, VROWS, wide), jnp.float32),
            pltpu.VMEM((tiles, 8, wide), jnp.float32),
            pltpu.SMEM((tiles,), jnp.int32),
            pltpu.VMEM((Y, CHUNKS, HALF if shared else TOK, HD), jnp.bfloat16),
            pltpu.VMEM((CHUNKS, KT, HD), jnp.bfloat16),
            pltpu.SemaphoreType.DMA((Y + 3 * X * (2 if shared else 1),)),
        ],
        compiler_params=pltpu.CompilerParams(vmem_limit_bytes=(20 if shared else 28) * 1024 * 1024),
        cost_estimate=pl.CostEstimate(flops=8 * pairs * HD, bytes_accessed=4 << 20, transcendentals=pairs),
        name="attend_shared" if shared else "attend_own",
    )(span_tiles, *arrays)


def turn(array, axis, size, by):
    return lax.ppermute(array, axis, [(i, (i + by) % size) for i in range(size)])


def after(array, *earlier):
    return lax.optimization_barrier((array, *earlier))[0]


def along_z(array):
    return lax.all_to_all(array, ("z", "c"), split_axis=0, concat_axis=0, tiled=True)


def combine(outs):
    tiles = outs[0].shape[0] // (TOK + 2)
    rows = tiles * TOK
    stats = []
    for item in outs:
        three = item[rows:].astype(jnp.float32)
        stats.append(three[:tiles, :TOK] + three[:tiles, TOK:] + three[tiles:, :TOK])
    top = jnp.maximum(jnp.maximum(stats[0], stats[1]), jnp.maximum(stats[2], stats[3]))
    weights = [jnp.exp2(item - top) for item in stats]
    total = weights[0] + weights[1] + weights[2] + weights[3]
    mixed = sum(
        (w / total)[:, :, None] * item[:rows].reshape(tiles, TOK, HD).astype(jnp.float32)
        for w, item in zip(weights, outs)
    )
    return mixed.astype(jnp.bfloat16).reshape(CHUNKS, -1, HD)


def body(queries, keys, values, span_tiles):
    def spread(array):
        return [turn(array, "x", X, d) for d in range(1, X)]

    def exchange(out):
        return [out[0]] + [turn(out[d], ("yh", "yl"), Y, -d) for d in range(1, Y)]

    most, rest = pack(queries, keys, values)
    most = along_z(most)
    rest = along_z(after(rest, most))
    mine = [most] + spread(most[:, :2 * TOK])
    q = most[:, 2 * TOK:]
    qs = [q] + [turn(q, ("yh", "yl"), Y, d) for d in range(1, Y - 1)]
    qs.append(turn(after(q, qs[1]), ("yh", "yl"), Y, Y - 1))
    mine2 = lax.all_to_all(
        jnp.broadcast_to(rest, (X, *rest.shape)), "x", split_axis=0, concat_axis=0, tiled=True
    )
    own_out = attend(span_tiles, False, qs, mine)
    others = lax.ppermute(after(mine2, own_out), "c", [(0, 1), (1, 0)])
    got = exchange(own_out)
    shared_out = attend(span_tiles, True, qs, [mine2, others])
    mixed = combine(after(got, shared_out))
    mixed2 = combine(exchange(shared_out))
    return unpack(along_z(jnp.concatenate([mixed, mixed2], axis=1)))


def solution(mesh):
    fine = Mesh(mesh.devices.reshape(Z, YH, CORES, YL, X), ALL)
    return jax.shard_map(
        body,
        mesh=fine,
        in_specs=(P(ALL, None), P(ALL, None), P(ALL, None), P()),
        out_specs=P(ALL, None),
        check_vma=False,
    )
```

```python
import functools

import jax
import jax.numpy as jnp
from jax import lax
from jax.experimental import pallas as pl
from jax.experimental.pallas import tpu as pltpu
from jax.sharding import Mesh, PartitionSpec as P

HD = 128
TILE = 128
SPANS = 4
Z, YH, CORES, YL, X = 8, 2, 2, 2, 4
Y = YH * YL
TOK = 64
HALF = TOK // 2
HEADS_HERE = 3
QT = Y * TOK
KT = X * TOK
PLANES = 4
CHUNKS = Z * CORES
GROUP = 4
VROWS = HD + 16
LOW = -1e30
FLOOR = -1e20
FACTOR = HD ** (-0.5) * 1.4426950408889634
ALL = ("z", "yh", "c", "yl", "x")


def pack_kernel(q_ref, k_ref, v_ref, most, rest):
    for plane in range(PLANES):
        for core in range(CORES):
            to = plane * CORES + core
            half = slice(core * HALF, (core + 1) * HALF)
            shared = slice(plane * HEADS_HERE * HD, (plane * HEADS_HERE + 1) * HD)
            lo = (plane * HEADS_HERE + 1 + core) * HD
            own = slice(lo, lo + HD)
            most[to, 0:TOK, :] = k_ref[:, own]
            most[to, TOK:2 * TOK, :] = v_ref[:, own]
            most[to, 2 * TOK:3 * TOK, :] = q_ref[:, own]
            most[to, 3 * TOK:3 * TOK + HALF, :] = q_ref[half, shared]
            rest[to, 0:HALF, :] = k_ref[half, shared]
            rest[to, HALF:TOK, :] = v_ref[half, shared]


def pack(queries, keys, values):
    blocks = [(PLANES * CORES, 3 * TOK + HALF, HD), (PLANES * CORES, TOK, HD)]
    return pl.pallas_call(
        pack_kernel,
        grid=(Z // PLANES,),
        in_specs=[pl.BlockSpec((TOK, PLANES * HEADS_HERE * HD), lambda i: (0, i))] * 3,
        out_specs=[pl.BlockSpec(block, lambda i: (i, 0, 0)) for block in blocks],
        out_shape=[
            jax.ShapeDtypeStruct((CHUNKS, 3 * TOK + HALF, HD), jnp.bfloat16),
            jax.ShapeDtypeStruct((CHUNKS, TOK, HD), jnp.bfloat16),
        ],
        name="pack",
    )(queries, keys, values)


def unpack_kernel(ref, out):
    for plane in range(PLANES):
        for core in range(CORES):
            at = plane * CORES + core
            lo = (plane * HEADS_HERE + 1 + core) * HD
            out[:, lo:lo + HD] = ref[at, 0:TOK, :]
            lo = plane * HEADS_HERE * HD
            out[core * HALF:(core + 1) * HALF, lo:lo + HD] = ref[at, TOK:TOK + HALF, :]


def unpack(parts):
    return pl.pallas_call(
        unpack_kernel,
        grid=(Z // PLANES,),
        in_specs=[pl.BlockSpec((PLANES * CORES, TOK + HALF, HD), lambda i: (i, 0, 0))],
        out_specs=pl.BlockSpec((TOK, PLANES * HEADS_HERE * HD), lambda i: (0, i)),
        out_shape=jax.ShapeDtypeStruct((TOK, Z * HEADS_HERE * HD), jnp.bfloat16),
        name="unpack",
    )(parts)


def attend_kernel(shared, planes, join, span_tiles, *refs):
    qs, refs = refs[:Y], refs[Y:]
    mine, refs = (refs[:CORES], refs[CORES:]) if shared else (refs[:X], refs[X:])
    o_refs, refs = refs[:Y], refs[Y:]
    k_scr, v_scr, s_scr, q_scr, limit_scr, acc_scr, top_scr, steps, q_in, v_in, sems = refs
    x = lax.axis_index("x")
    y = lax.axis_index("yh") * YL + lax.axis_index("yl")
    bounds = [span_tiles[0] * TILE]
    for s in range(1, SPANS):
        bounds.append(bounds[-1] + span_tiles[s] * TILE)

    copies = [[], [], []]

    def fetch(kind, source, target):
        copy = pltpu.make_async_copy(source, target, sems.at[sum(map(len, copies))])
        copy.start()
        copies[kind].append(copy)

    for d in range(Y):
        at = pl.ds(TOK, HALF) if shared else pl.ds(0, TOK)
        fetch(0, qs[d].at[:, at, :], q_in.at[d])
    size = HALF if shared else TOK
    for d in range(X):
        sources = [ref.at[(x + X - d) % X] for ref in mine] if shared else [mine[d]]
        for e, source in enumerate(sources):
            at = pl.ds(d * TOK + e * HALF, size)
            fetch(1, source.at[:, pl.ds(size, size), :], v_in.at[:, at, :])
            for twice in range(2):
                fetch(2, source.at[:, pl.ds(0, size), :], k_scr.at[:, at, pl.ds(twice * HD, HD)])

    tiles = planes // join
    wide = join * QT
    ones = jnp.ones((VROWS - HD, KT), jnp.bfloat16)
    y_off = (y // YL) * (TOK * CORES * YL * X) + (y % YL) * KT
    lane = lax.broadcasted_iota(jnp.int32, (1, QT), 1)
    rows = planes * TOK

    def chunk_start(j):
        return (j // CORES) * (TOK * 32) + (j % CORES) * (TOK * 8) + y_off

    def arrange_values(m, carry):
        for g in range(GROUP):
            v_scr[m, 0:HD, g * KT:(g + 1) * KT] = v_in[m * GROUP + g].T
            v_scr[m, HD:VROWS, g * KT:(g + 1) * KT] = ones
        return carry

    def arrange_queries(t, whole):
        most = jnp.int32(0)
        for part in range(join):
            i = t * join + part
            parts = []
            for d in range(Y):
                if shared:
                    parts += [q_in[d, i * CORES + e] for e in range(CORES)]
                else:
                    parts.append(q_in[d, i])
            q = jnp.concatenate(parts, axis=0).astype(jnp.float32) * FACTOR
            high = q.astype(jnp.bfloat16)
            low = (q - high.astype(jnp.float32)).astype(jnp.bfloat16)
            at = slice(part * QT, (part + 1) * QT)
            q_scr[t, 0:HD, at] = high.T
            q_scr[t, HD:2 * HD, at] = low.T
            row = jnp.zeros((1, QT), jnp.int32)
            for block in range(QT // size):
                yq = (y + Y - (block * size) // TOK) % Y
                j = i * CORES + block % CORES if shared else i
                tok = (j // CORES) * (TOK * 32) + (yq // YL) * (TOK * 16) + (j % CORES) * (TOK * 8) + (yq % YL) * (TOK * 4) + x * TOK
                end = bounds[SPANS - 1]
                for s in range(SPANS - 2, -1, -1):
                    end = jnp.where(tok < bounds[s], bounds[s], end)
                most = jnp.maximum(most, end)
                row = jnp.where(lane >= block * size, end, row)
            limit_scr[t, 0:1, at] = row
        far = jnp.maximum(most - y_off, 0)
        rest = far % (TOK * 32)
        seen = (far // (TOK * 32)) * CORES + (rest > 0).astype(jnp.int32) + (rest > TOK * 8).astype(jnp.int32)
        count = jnp.maximum((seen + GROUP - 1) // GROUP, 1)
        steps[t] = count
        acc_scr[t] = jnp.zeros((VROWS, wide), jnp.float32)
        return whole + count

    for copy in copies[0]:
        copy.wait()
    rounds = lax.fori_loop(0, tiles, arrange_queries, jnp.int32(0))
    for copy in copies[1]:
        copy.wait()
    lax.fori_loop(0, CHUNKS // GROUP, arrange_values, 0)
    for copy in copies[2]:
        copy.wait()

    def bias_rows(t, j):
        start = chunk_start(j)
        limit_row = limit_scr[t, 0:1, :]
        return [jnp.where(start + ((x + X - d) % X) * TOK < limit_row, 0.0, LOW) for d in range(X)]

    def produce(t, j, slot, best):
        s = jnp.dot(k_scr[j], q_scr[t], preferred_element_type=jnp.float32)
        s_scr[slot] = s
        for d, bias in enumerate(bias_rows(t, j)):
            part = jnp.max(s[d * TOK:(d + 1) * TOK].reshape(TOK // 8, 8, wide), axis=0) + bias
            best = jnp.maximum(best, part)
        return best

    def produce_all(t, n, best):
        keys = k_scr[pl.ds(n * GROUP, GROUP)].reshape(GROUP * KT, 2 * HD)
        scores = jnp.dot(keys, q_scr[t], preferred_element_type=jnp.float32)
        for g in range(GROUP):
            s = scores[g * KT:(g + 1) * KT]
            s_scr[g] = s
            for d, bias in enumerate(bias_rows(t, n * GROUP + g)):
                part = jnp.max(s[d * TOK:(d + 1) * TOK].reshape(TOK // 8, 8, wide), axis=0) + bias
                best = jnp.maximum(best, part)
        return best

    def consume(t, j, slot, top):
        s = s_scr[slot]
        ps = []
        for d, bias in enumerate(bias_rows(t, j)):
            ps.append(jnp.exp2(s[d * TOK:(d + 1) * TOK] - (top - bias)).astype(jnp.bfloat16))
        return jnp.concatenate(ps, axis=0)

    def step(_, state):
        t, n, best, old = state
        top = jnp.max(best, axis=0, keepdims=True)
        last = n + 1 >= steps[t]
        t2 = jnp.where(last, jnp.minimum(t + 1, tiles - 1), t)
        n2 = jnp.where(last, 0, n + 1)
        best = jnp.where(last, FLOOR, best)
        accum = acc_scr[t] * jnp.exp2(old - top)
        ps = []
        for g in range(GROUP):
            j = n * GROUP + g
            p = consume(t, j, g, top)
            ps.append(p)
            if not shared:
                best = produce(t2, n2 * GROUP + g, g, best)
        if shared:
            best = produce_all(t2, n2, best)
        acc_scr[t] = accum + jnp.dot(v_scr[n], jnp.concatenate(ps, axis=0), preferred_element_type=jnp.float32)
        top_scr[t, 0:1, :] = top
        return t2, n2, best, jnp.where(last, FLOOR, top)

    best = jnp.full((8, wide), FLOOR, jnp.float32)
    for g in range(GROUP):
        best = produce(0, g, g, best)
    lax.fori_loop(0, rounds, step, (jnp.int32(0), jnp.int32(0), best, jnp.full((1, wide), FLOOR, jnp.float32)))
    stats = []
    for i in range(planes):
        t, at = i // join, slice(i % join * QT, (i % join + 1) * QT)
        total = acc_scr[t, HD:HD + 1, at]
        some = total > 0.0
        safe = jnp.where(some, total, 1.0)
        stats.append(jnp.where(some, top_scr[t, 0:1, at] + jnp.log2(safe), LOW))
        out = (acc_scr[t, 0:HD, at] * (1.0 / safe)).T.astype(jnp.bfloat16)
        for d in range(Y):
            o_refs[d][i * TOK:(i + 1) * TOK, :] = out[d * TOK:(d + 1) * TOK]
    lse = jnp.concatenate(stats, axis=0)
    high = lse.astype(jnp.bfloat16)
    lse = lse - high.astype(jnp.float32)
    middle = lse.astype(jnp.bfloat16)
    low = (lse - middle.astype(jnp.float32)).astype(jnp.bfloat16)
    for d in range(Y):
        at = slice(d * TOK, (d + 1) * TOK)
        first = jnp.concatenate([high[:, at], middle[:, at]], axis=1)
        second = jnp.concatenate([low[:, at], jnp.zeros((planes, HD - TOK), jnp.bfloat16)], axis=1)
        o_refs[d][rows:rows + 2 * planes, :] = jnp.concatenate([first, second], axis=0)


def attend(span_tiles, shared, qs, mine):
    planes = Z if shared else CHUNKS
    join = 2 if shared else 4
    tiles, wide = planes // join, join * QT
    pairs = planes * QT * CHUNKS * KT
    arrays = [*qs, *mine]
    return pl.pallas_call(
        functools.partial(attend_kernel, shared, planes, join),
        in_specs=[pl.BlockSpec(memory_space=pltpu.SMEM)] + [pl.BlockSpec(memory_space=pl.ANY)] * len(arrays),
        out_specs=[pl.BlockSpec(memory_space=pltpu.VMEM)] * Y,
        out_shape=[pltpu.VMEM((planes * (TOK + 2), HD), jnp.bfloat16)] * Y,
        scratch_shapes=[
            pltpu.VMEM((CHUNKS, KT, 2 * HD), jnp.bfloat16),
            pltpu.VMEM((CHUNKS // GROUP, VROWS, GROUP * KT), jnp.bfloat16),
            pltpu.VMEM((GROUP, KT, wide), jnp.float32),
            pltpu.VMEM((tiles, 2 * HD, wide), jnp.bfloat16),
            pltpu.VMEM((tiles, 8, wide), jnp.int32),
            pltpu.VMEM((tiles, VROWS, wide), jnp.float32),
            pltpu.VMEM((tiles, 8, wide), jnp.float32),
            pltpu.SMEM((tiles,), jnp.int32),
            pltpu.VMEM((Y, CHUNKS, HALF if shared else TOK, HD), jnp.bfloat16),
            pltpu.VMEM((CHUNKS, KT, HD), jnp.bfloat16),
            pltpu.SemaphoreType.DMA((Y + 3 * X * (2 if shared else 1),)),
        ],
        compiler_params=pltpu.CompilerParams(vmem_limit_bytes=(20 if shared else 28) * 1024 * 1024),
        cost_estimate=pl.CostEstimate(flops=8 * pairs * HD, bytes_accessed=4 << 20, transcendentals=pairs),
        name="attend_shared" if shared else "attend_own",
    )(span_tiles, *arrays)


def turn(array, axis, size, by):
    return lax.ppermute(array, axis, [(i, (i + by) % size) for i in range(size)])


def after(array, *earlier):
    return lax.optimization_barrier((array, *earlier))[0]


def along_z(array):
    return lax.all_to_all(array, ("z", "c"), split_axis=0, concat_axis=0, tiled=True)


def combine(outs):
    tiles = outs[0].shape[0] // (TOK + 2)
    rows = tiles * TOK
    stats = []
    for item in outs:
        three = item[rows:].astype(jnp.float32)
        stats.append(three[:tiles, :TOK] + three[:tiles, TOK:] + three[tiles:, :TOK])
    top = jnp.maximum(jnp.maximum(stats[0], stats[1]), jnp.maximum(stats[2], stats[3]))
    weights = [jnp.exp2(item - top) for item in stats]
    total = weights[0] + weights[1] + weights[2] + weights[3]
    mixed = sum(
        (w / total)[:, :, None] * item[:rows].reshape(tiles, TOK, HD).astype(jnp.float32)
        for w, item in zip(weights, outs)
    )
    return mixed.astype(jnp.bfloat16).reshape(CHUNKS, -1, HD)


def body(queries, keys, values, span_tiles):
    def spread(array):
        return [turn(array, "x", X, d) for d in range(1, X)]

    def exchange(out):
        return [out[0]] + [turn(out[d], ("yh", "yl"), Y, -d) for d in range(1, Y)]

    most, rest = pack(queries, keys, values)
    most = along_z(most)
    rest = along_z(after(rest, most))
    mine = [most] + spread(most[:, :2 * TOK])
    q = most[:, 2 * TOK:]
    far = turn(q, ("yh", "yl"), Y, 2)
    qs = [q, turn(q, ("yh", "yl"), Y, 1), far, turn(after(q, far), ("yh", "yl"), Y, 3)]
    mine2 = lax.all_to_all(
        jnp.broadcast_to(rest, (X, *rest.shape)), "x", split_axis=0, concat_axis=0, tiled=True
    )
    own_out = attend(span_tiles, False, qs, mine)
    others = lax.ppermute(after(mine2, own_out), "c", [(0, 1), (1, 0)])
    got = exchange(own_out)
    shared_out = attend(span_tiles, True, qs, [mine2, others])
    mixed = combine(after(got, shared_out))
    mixed2 = combine(exchange(shared_out))
    return unpack(along_z(jnp.concatenate([mixed, mixed2], axis=1)))


def solution(mesh):
    fine = Mesh(mesh.devices.reshape(Z, YH, CORES, YL, X), ALL)
    return jax.shard_map(
        body,
        mesh=fine,
        in_specs=(P(ALL, None), P(ALL, None), P(ALL, None), P()),
        out_specs=P(ALL, None),
        check_vma=False,
    )
```

```python
import functools

import jax
import jax.numpy as jnp
from jax import lax
from jax.experimental import pallas as pl
from jax.experimental.pallas import tpu as pltpu
from jax.sharding import Mesh, PartitionSpec as P

HD = 128
TILE = 128
SPANS = 4
Z, YH, CORES, YL, X = 8, 2, 2, 2, 4
Y = YH * YL
TOK = 64
HALF = TOK // 2
HEADS_HERE = 3
QT = Y * TOK
KT = X * TOK
PLANES = 2
CHUNKS = Z * CORES
GROUP = 4
VROWS = HD + 16
LOW = -1e30
FLOOR = -1e20
FACTOR = HD ** (-0.5) * 1.4426950408889634
ALL = ("z", "yh", "c", "yl", "x")


def pack_kernel(q_ref, k_ref, v_ref, most, rest):
    for plane in range(PLANES):
        for core in range(CORES):
            to = plane * CORES + core
            half = slice(core * HALF, (core + 1) * HALF)
            shared = slice(plane * HEADS_HERE * HD, (plane * HEADS_HERE + 1) * HD)
            lo = (plane * HEADS_HERE + 1 + core) * HD
            own = slice(lo, lo + HD)
            most[to, 0:TOK, :] = k_ref[:, own]
            most[to, TOK:2 * TOK, :] = v_ref[:, own]
            most[to, 2 * TOK:3 * TOK, :] = q_ref[:, own]
            most[to, 3 * TOK:3 * TOK + HALF, :] = q_ref[half, shared]
            rest[to, 0:HALF, :] = k_ref[half, shared]
            rest[to, HALF:TOK, :] = v_ref[half, shared]


def pack(queries, keys, values):
    blocks = [(PLANES * CORES, 3 * TOK + HALF, HD), (PLANES * CORES, TOK, HD)]
    return pl.pallas_call(
        pack_kernel,
        grid=(Z // PLANES,),
        in_specs=[pl.BlockSpec((TOK, PLANES * HEADS_HERE * HD), lambda i: (0, i))] * 3,
        out_specs=[pl.BlockSpec(block, lambda i: (i, 0, 0)) for block in blocks],
        out_shape=[
            jax.ShapeDtypeStruct((CHUNKS, 3 * TOK + HALF, HD), jnp.bfloat16),
            jax.ShapeDtypeStruct((CHUNKS, TOK, HD), jnp.bfloat16),
        ],
        name="pack",
    )(queries, keys, values)


def unpack_kernel(ref, out):
    for plane in range(PLANES):
        for core in range(CORES):
            at = plane * CORES + core
            lo = (plane * HEADS_HERE + 1 + core) * HD
            out[:, lo:lo + HD] = ref[at, 0:TOK, :]
            lo = plane * HEADS_HERE * HD
            out[core * HALF:(core + 1) * HALF, lo:lo + HD] = ref[at, TOK:TOK + HALF, :]


def unpack(parts):
    return pl.pallas_call(
        unpack_kernel,
        grid=(Z // PLANES,),
        in_specs=[pl.BlockSpec((PLANES * CORES, TOK + HALF, HD), lambda i: (i, 0, 0))],
        out_specs=pl.BlockSpec((TOK, PLANES * HEADS_HERE * HD), lambda i: (0, i)),
        out_shape=jax.ShapeDtypeStruct((TOK, Z * HEADS_HERE * HD), jnp.bfloat16),
        name="unpack",
    )(parts)


def attend_kernel(shared, planes, join, span_tiles, *refs):
    qs, refs = refs[:Y], refs[Y:]
    mine, refs = (refs[:CORES], refs[CORES:]) if shared else (refs[:X], refs[X:])
    o_refs, refs = refs[:Y], refs[Y:]
    k_scr, v_scr, s_scr, q_scr, limit_scr, acc_scr, top_scr, steps, q_in, v_in, sems = refs
    x = lax.axis_index("x")
    y = lax.axis_index("yh") * YL + lax.axis_index("yl")
    bounds = [span_tiles[0] * TILE]
    for s in range(1, SPANS):
        bounds.append(bounds[-1] + span_tiles[s] * TILE)

    copies = [[], [], []]

    def fetch(kind, source, target):
        copy = pltpu.make_async_copy(source, target, sems.at[sum(map(len, copies))])
        copy.start()
        copies[kind].append(copy)

    for d in range(Y):
        at = pl.ds(TOK, HALF) if shared else pl.ds(0, TOK)
        fetch(0, qs[d].at[:, at, :], q_in.at[d])
    size = HALF if shared else TOK
    for d in range(X):
        sources = [ref.at[(x + X - d) % X] for ref in mine] if shared else [mine[d]]
        for e, source in enumerate(sources):
            at = pl.ds(d * TOK + e * HALF, size)
            fetch(1, source.at[:, pl.ds(size, size), :], v_in.at[:, at, :])
            for twice in range(2):
                fetch(2, source.at[:, pl.ds(0, size), :], k_scr.at[:, at, pl.ds(twice * HD, HD)])

    tiles = planes // join
    wide = join * QT
    ones = jnp.ones((VROWS - HD, KT), jnp.bfloat16)
    y_off = (y // YL) * (TOK * CORES * YL * X) + (y % YL) * KT
    lane = lax.broadcasted_iota(jnp.int32, (1, QT), 1)
    rows = planes * TOK

    def chunk_start(j):
        return (j // CORES) * (TOK * 32) + (j % CORES) * (TOK * 8) + y_off

    def arrange_values(m, carry):
        for g in range(GROUP):
            v_scr[m, 0:HD, g * KT:(g + 1) * KT] = v_in[m * GROUP + g].T
            v_scr[m, HD:VROWS, g * KT:(g + 1) * KT] = ones
        return carry

    def arrange_queries(t, whole):
        most = jnp.int32(0)
        for part in range(join):
            i = t * join + part
            parts = []
            for d in range(Y):
                if shared:
                    parts += [q_in[d, i * CORES + e] for e in range(CORES)]
                else:
                    parts.append(q_in[d, i])
            q = jnp.concatenate(parts, axis=0).astype(jnp.float32) * FACTOR
            high = q.astype(jnp.bfloat16)
            low = (q - high.astype(jnp.float32)).astype(jnp.bfloat16)
            at = slice(part * QT, (part + 1) * QT)
            q_scr[t, 0:HD, at] = high.T
            q_scr[t, HD:2 * HD, at] = low.T
            row = jnp.zeros((1, QT), jnp.int32)
            for block in range(QT // size):
                yq = (y + Y - (block * size) // TOK) % Y
                j = i * CORES + block % CORES if shared else i
                tok = (j // CORES) * (TOK * 32) + (yq // YL) * (TOK * 16) + (j % CORES) * (TOK * 8) + (yq % YL) * (TOK * 4) + x * TOK
                end = bounds[SPANS - 1]
                for s in range(SPANS - 2, -1, -1):
                    end = jnp.where(tok < bounds[s], bounds[s], end)
                most = jnp.maximum(most, end)
                row = jnp.where(lane >= block * size, end, row)
            limit_scr[t, 0:1, at] = row
        far = jnp.maximum(most - y_off, 0)
        rest = far % (TOK * 32)
        seen = (far // (TOK * 32)) * CORES + (rest > 0).astype(jnp.int32) + (rest > TOK * 8).astype(jnp.int32)
        count = jnp.maximum((seen + GROUP - 1) // GROUP, 1)
        steps[t] = count
        acc_scr[t] = jnp.zeros((VROWS, wide), jnp.float32)
        return whole + count

    for copy in copies[0]:
        copy.wait()
    rounds = lax.fori_loop(0, tiles, arrange_queries, jnp.int32(0))
    for copy in copies[1]:
        copy.wait()
    lax.fori_loop(0, CHUNKS // GROUP, arrange_values, 0)
    for copy in copies[2]:
        copy.wait()

    def bias_rows(t, j):
        start = chunk_start(j)
        limit_row = limit_scr[t, 0:1, :]
        return [jnp.where(start + ((x + X - d) % X) * TOK < limit_row, 0.0, LOW) for d in range(X)]

    def produce(t, j, slot, best):
        s = jnp.dot(k_scr[j], q_scr[t], preferred_element_type=jnp.float32)
        s_scr[slot] = s
        for d, bias in enumerate(bias_rows(t, j)):
            part = jnp.max(s[d * TOK:(d + 1) * TOK].reshape(TOK // 8, 8, wide), axis=0) + bias
            best = jnp.maximum(best, part)
        return best

    def produce_all(t, n, best):
        keys = k_scr[pl.ds(n * GROUP, GROUP)].reshape(GROUP * KT, 2 * HD)
        scores = jnp.dot(keys, q_scr[t], preferred_element_type=jnp.float32)
        for g in range(GROUP):
            s = scores[g * KT:(g + 1) * KT]
            s_scr[g] = s
            for d, bias in enumerate(bias_rows(t, n * GROUP + g)):
                part = jnp.max(s[d * TOK:(d + 1) * TOK].reshape(TOK // 8, 8, wide), axis=0) + bias
                best = jnp.maximum(best, part)
        return best

    def consume(t, j, slot, top):
        s = s_scr[slot]
        ps = []
        for d, bias in enumerate(bias_rows(t, j)):
            ps.append(jnp.exp2(s[d * TOK:(d + 1) * TOK] - (top - bias)).astype(jnp.bfloat16))
        return jnp.concatenate(ps, axis=0)

    def step(_, state):
        t, n, best, old = state
        top = jnp.max(best, axis=0, keepdims=True)
        last = n + 1 >= steps[t]
        t2 = jnp.where(last, jnp.minimum(t + 1, tiles - 1), t)
        n2 = jnp.where(last, 0, n + 1)
        best = jnp.where(last, FLOOR, best)
        accum = acc_scr[t] * jnp.exp2(old - top)
        ps = []
        for g in range(GROUP):
            j = n * GROUP + g
            p = consume(t, j, g, top)
            ps.append(p)
            if not shared:
                best = produce(t2, n2 * GROUP + g, g, best)
        if shared:
            best = produce_all(t2, n2, best)
        acc_scr[t] = accum + jnp.dot(v_scr[n], jnp.concatenate(ps, axis=0), preferred_element_type=jnp.float32)
        top_scr[t, 0:1, :] = top
        return t2, n2, best, jnp.where(last, FLOOR, top)

    best = jnp.full((8, wide), FLOOR, jnp.float32)
    for g in range(GROUP):
        best = produce(0, g, g, best)
    lax.fori_loop(0, rounds, step, (jnp.int32(0), jnp.int32(0), best, jnp.full((1, wide), FLOOR, jnp.float32)))
    stats = []
    for i in range(planes):
        t, at = i // join, slice(i % join * QT, (i % join + 1) * QT)
        total = acc_scr[t, HD:HD + 1, at]
        some = total > 0.0
        safe = jnp.where(some, total, 1.0)
        stats.append(jnp.where(some, top_scr[t, 0:1, at] + jnp.log2(safe), LOW))
        out = (acc_scr[t, 0:HD, at] * (1.0 / safe)).T.astype(jnp.bfloat16)
        for d in range(Y):
            o_refs[d][i * TOK:(i + 1) * TOK, :] = out[d * TOK:(d + 1) * TOK]
    lse = jnp.concatenate(stats, axis=0)
    high = lse.astype(jnp.bfloat16)
    lse = lse - high.astype(jnp.float32)
    middle = lse.astype(jnp.bfloat16)
    low = (lse - middle.astype(jnp.float32)).astype(jnp.bfloat16)
    for d in range(Y):
        at = slice(d * TOK, (d + 1) * TOK)
        first = jnp.concatenate([high[:, at], middle[:, at]], axis=1)
        second = jnp.concatenate([low[:, at], jnp.zeros((planes, HD - TOK), jnp.bfloat16)], axis=1)
        o_refs[d][rows:rows + 2 * planes, :] = jnp.concatenate([first, second], axis=0)


def attend(span_tiles, shared, qs, mine):
    planes = Z if shared else CHUNKS
    join = 2 if shared else 4
    tiles, wide = planes // join, join * QT
    pairs = planes * QT * CHUNKS * KT
    arrays = [*qs, *mine]
    return pl.pallas_call(
        functools.partial(attend_kernel, shared, planes, join),
        in_specs=[pl.BlockSpec(memory_space=pltpu.SMEM)] + [pl.BlockSpec(memory_space=pl.ANY)] * len(arrays),
        out_specs=[pl.BlockSpec(memory_space=pltpu.VMEM)] * Y,
        out_shape=[pltpu.VMEM((planes * (TOK + 2), HD), jnp.bfloat16)] * Y,
        scratch_shapes=[
            pltpu.VMEM((CHUNKS, KT, 2 * HD), jnp.bfloat16),
            pltpu.VMEM((CHUNKS // GROUP, VROWS, GROUP * KT), jnp.bfloat16),
            pltpu.VMEM((GROUP, KT, wide), jnp.float32),
            pltpu.VMEM((tiles, 2 * HD, wide), jnp.bfloat16),
            pltpu.VMEM((tiles, 8, wide), jnp.int32),
            pltpu.VMEM((tiles, VROWS, wide), jnp.float32),
            pltpu.VMEM((tiles, 8, wide), jnp.float32),
            pltpu.SMEM((tiles,), jnp.int32),
            pltpu.VMEM((Y, CHUNKS, HALF if shared else TOK, HD), jnp.bfloat16),
            pltpu.VMEM((CHUNKS, KT, HD), jnp.bfloat16),
            pltpu.SemaphoreType.DMA((Y + 3 * X * (2 if shared else 1),)),
        ],
        compiler_params=pltpu.CompilerParams(vmem_limit_bytes=(20 if shared else 28) * 1024 * 1024),
        cost_estimate=pl.CostEstimate(flops=8 * pairs * HD, bytes_accessed=4 << 20, transcendentals=pairs),
        name="attend_shared" if shared else "attend_own",
    )(span_tiles, *arrays)


def turn(array, axis, size, by):
    return lax.ppermute(array, axis, [(i, (i + by) % size) for i in range(size)])


def after(array, *earlier):
    return lax.optimization_barrier((array, *earlier))[0]


def along_z(array):
    return lax.all_to_all(array, ("z", "c"), split_axis=0, concat_axis=0, tiled=True)


def combine(outs):
    tiles = outs[0].shape[0] // (TOK + 2)
    rows = tiles * TOK
    stats = []
    for item in outs:
        three = item[rows:].astype(jnp.float32)
        stats.append(three[:tiles, :TOK] + three[:tiles, TOK:] + three[tiles:, :TOK])
    top = jnp.maximum(jnp.maximum(stats[0], stats[1]), jnp.maximum(stats[2], stats[3]))
    weights = [jnp.exp2(item - top) for item in stats]
    total = weights[0] + weights[1] + weights[2] + weights[3]
    mixed = sum(
        (w / total)[:, :, None] * item[:rows].reshape(tiles, TOK, HD).astype(jnp.float32)
        for w, item in zip(weights, outs)
    )
    return mixed.astype(jnp.bfloat16).reshape(CHUNKS, -1, HD)


def body(queries, keys, values, span_tiles):
    def spread(array):
        return [turn(array, "x", X, d) for d in range(1, X)]

    def exchange(out):
        far = turn(out[2], ("yh", "yl"), Y, -2)
        return [out[0], far] + [turn(out[d], ("yh", "yl"), Y, -d) for d in (1, 3)]

    most, rest = pack(queries, keys, values)
    most = along_z(most)
    rest = along_z(after(rest, most))
    mine = [most] + spread(most[:, :2 * TOK])
    q = most[:, 2 * TOK:]
    far = turn(q, ("yh", "yl"), Y, 2)
    qs = [q, turn(q, ("yh", "yl"), Y, 1), far, turn(after(q, far), ("yh", "yl"), Y, 3)]
    mine2 = lax.all_to_all(
        jnp.broadcast_to(rest, (X, *rest.shape)), "x", split_axis=0, concat_axis=0, tiled=True
    )
    own_out = attend(span_tiles, False, qs, mine)
    others = lax.ppermute(after(mine2, own_out), "c", [(0, 1), (1, 0)])
    got = exchange(own_out)
    shared_out = attend(span_tiles, True, qs, [mine2, others])
    mixed = combine(after(got, shared_out))
    mixed2 = combine(exchange(shared_out))
    return unpack(along_z(jnp.concatenate([mixed, mixed2], axis=1)))


def solution(mesh):
    fine = Mesh(mesh.devices.reshape(Z, YH, CORES, YL, X), ALL)
    return jax.shard_map(
        body,
        mesh=fine,
        in_specs=(P(ALL, None), P(ALL, None), P(ALL, None), P()),
        out_specs=P(ALL, None),
        check_vma=False,
    )
```
